32 devices in a mesh: seq: 8 (over y, x, core), head: 4 (over z).
Axes of the slice: x: 2, y: 2, z: 4, core: 2. Of those that a mesh axis runs over, the one named last changes fastest.
Arguments:
- queries: bfloat16 [1024, 8192], P('seq', 'head'), may hold values from -6 to 6, as said below
- keys: bfloat16 [1024, 1024], P('seq'), may hold values from -6 to 6, as said below
- values: bfloat16 [1024, 1024], P('seq'), may hold values from -6 to 6
- residual: bfloat16 [1024, 8192], P('seq', 'head'), may hold values from -50 to 50
- norm_gain: float32 [8192], replicated, may hold values from 0.25 to 1.75
- block_pos: int32 [1, 8], replicated, may hold values from 0 to 7, each once within a row
- doc_offset: int32 [1, 8], replicated, may hold values from 1 to 128, as said below
Outputs:
- attn_out: bfloat16 [1024, 8192], P('seq', 'head')
- r_factor: float32 [64, 128, 128], P('head')
- whitened: float32 [1024, 8192], P('seq', 'head')
The draws below stay inside these ranges and needn't reach their ends.
Inputs may be any that keep to these rules, and one draw needn't show every extreme that they name: queries may hold rows of large entries. keys may hold rows of large entries. `block_pos`: in each sequence every sequence block is stored exactly once. A document begins at token doc_offset[c, b] of sequence block b when that value is under 128; the first document begins at position 0.
All inputs are finite; a program needn't handle non-finite values.
Results may differ from the reference program's by a relative error of at most 0.0045.
Values may be sent and summed in bfloat16 or wider, within the bound.
A program may use at most 64 MiB of HBM per device.

```python
import math
import jax
import jax.numpy as jnp
from jax import lax

HEADS = 64
KVH = 8
HD = 128
BLOCK = 128
COPIES = 1
TOKENS = 1024
NBLK = 8
WIDTH = 8192


def draw_queries(key, part):
    sample_key = jax.random.fold_in(key, 1)
    columns = COPIES * HEADS * HD
    result = jnp.clip(jax.random.normal(sample_key, (TOKENS, columns), jnp.float32), -6.0, 6.0)
    return result.astype(jnp.bfloat16)


def draw_keys(key, part):
    sample_key = jax.random.fold_in(key, 2)
    columns = COPIES * KVH * HD
    result = jnp.clip(jax.random.normal(sample_key, (TOKENS, columns), jnp.float32), -6.0, 6.0)
    return result.astype(jnp.bfloat16)


def draw_residual(key, part):
    columns = COPIES * WIDTH
    row_scale = jnp.exp(jax.random.uniform(jax.random.fold_in(key, 31), (TOKENS,), jnp.float32, math.log(0.1), 0.0))
    place = (jnp.arange(columns, dtype=jnp.int32) % WIDTH).astype(jnp.float32)
    column_rise = jnp.exp(math.log(10.0) * place / (WIDTH - 1))
    column_jitter = jnp.exp(jax.random.uniform(jax.random.fold_in(key, 32), (columns,), jnp.float32, -0.5, 0.5))
    sample_key = jax.random.fold_in(key, 33)
    base = jax.random.normal(sample_key, (TOKENS, columns), jnp.float32)
    base = jnp.clip(base, -6.0, 6.0)
    return (0.5 * base * row_scale[:, None] * (column_rise * column_jitter)[None, :]).astype(jnp.bfloat16)


def draw_doc_offset(key, part):
    starting = jax.random.randint(jax.random.fold_in(key, 21), (COPIES, NBLK), 0, 8) == 0
    placed = jax.random.randint(jax.random.fold_in(key, 22), (COPIES, NBLK), 1, BLOCK)
    result = jnp.where(starting, placed, BLOCK)
    result = result.at[:, 0].set(BLOCK)
    return result.astype(jnp.int32)


def level_of(own_key, shape, cuts, smallest, top_value):
    loudness = 1.0
    for position, parts in cuts:
        steps = jax.random.uniform(jax.random.fold_in(jax.random.fold_in(own_key, 6), position), (parts,), jnp.float32, smallest / len(cuts), top_value / len(cuts))
        loudness = loudness * jnp.repeat(jnp.exp(steps), shape[position] // parts).reshape((-1,) + (1,) * (len(shape) - 1 - position))
    return loudness


def centred(key, dims, deviation, most, split=(), kind=jnp.bfloat16):
    entries = jax.random.normal(key, dims, jnp.float32) * deviation
    if len(split) > 0:
        entries = level_of(key, dims, split, -0.22, 0.18) * entries
    return jnp.clip(entries, min=-most, max=most).astype(kind)


def setup_inputs(seed: int = 0) -> dict:
    splits = jax.random.split(jax.random.key(seed), 8)
    return {
        "queries": draw_queries(jax.random.fold_in(splits[7], 71), 0),
        "keys": draw_keys(jax.random.fold_in(splits[7], 71), 0),
        "values": centred(splits[2], (TOKENS, COPIES * KVH * HD), 1.0, 6.0, ((0, 8),)),
        "residual": draw_residual(jax.random.fold_in(splits[7], 71), 0),
        "norm_gain": jnp.clip(1.0 + 0.15 * jax.random.normal(splits[4], (WIDTH,), jnp.float32), 0.25, 1.75),
        "block_pos": jax.vmap(lambda own: jax.random.permutation(own, NBLK))(jax.random.split(splits[5], COPIES)).reshape((COPIES, NBLK)).astype(jnp.int32),
        "doc_offset": draw_doc_offset(jax.random.fold_in(splits[7], 71), 0),
    }


EPSILON = 1e-05

def positions_and_docs(block_pos, doc_offset):
    block_total = block_pos.shape[0]
    doc_flags = (doc_offset < BLOCK).astype(jnp.int32)
    starts_before = (jnp.cumsum(doc_flags) - doc_flags).astype(jnp.int32)
    matches = block_pos[:, None] == jnp.arange(block_total, dtype=jnp.int32)[None, :]
    start_count = lax.optimization_barrier(jnp.sum(jnp.where(matches, starts_before[None, :], 0), axis=1)).astype(jnp.int32)
    offsets = lax.optimization_barrier(jnp.sum(jnp.where(matches, doc_offset[None, :], 0), axis=1)).astype(jnp.int32)
    within = jnp.arange(BLOCK, dtype=jnp.int32)
    seq_pos = (block_pos[:, None] * BLOCK + within[None, :]).reshape(-1).astype(jnp.int32)
    doc_id = (start_count[:, None] + (within[None, :] >= offsets[:, None]).astype(jnp.int32)).reshape(-1)
    return (seq_pos, doc_id.astype(jnp.int32))

def one_sequence(queries, keys, values, residual, norm_gain, block_pos, doc_offset):
    seq_pos, doc_id = positions_and_docs(block_pos, doc_offset)
    visible = (seq_pos[None, :] <= seq_pos[:, None]) & (doc_id[None, :] == doc_id[:, None])
    group_size = HEADS // KVH
    score_scale = 1.0 / math.sqrt(HD)

    def one_head(head_index):
        query_cols = lax.dynamic_slice_in_dim(queries, head_index * HD, HD, 1)
        share = head_index // group_size
        key_cols = lax.dynamic_slice_in_dim(keys, share * HD, HD, 1)
        value_cols = lax.dynamic_slice_in_dim(values, share * HD, HD, 1)
        scores = jnp.dot(query_cols.astype(jnp.float32), key_cols.T.astype(jnp.float32), preferred_element_type=jnp.float32) * score_scale
        scores = jnp.where(visible, scores, -jnp.inf)
        row_max = lax.optimization_barrier(jnp.max(scores, axis=1, keepdims=True))
        expo = jnp.exp(scores - row_max)
        totals = lax.optimization_barrier(jnp.sum(expo, axis=1, keepdims=True))
        output = jnp.dot(expo.astype(jnp.bfloat16).astype(jnp.float32), value_cols.astype(jnp.float32), preferred_element_type=jnp.float32) / totals
        return output.astype(jnp.bfloat16)
    per_head = lax.map(one_head, jnp.arange(HEADS, dtype=jnp.int32))
    attn_out = jnp.transpose(per_head, (1, 0, 2)).reshape(TOKENS, WIDTH)
    mixed = attn_out.astype(jnp.float32) + residual.astype(jnp.float32)
    square_sum = lax.optimization_barrier(jnp.sum(mixed * mixed, axis=1, keepdims=True))
    normed = mixed * lax.rsqrt(square_sum / WIDTH + EPSILON) * norm_gain[None, :]
    blocks = normed.reshape(TOKENS, HEADS, HD)
    gram_sum = jnp.einsum('rhc,rhd->hcd', blocks, blocks, precision=lax.Precision.HIGHEST)
    lower_factor = jnp.linalg.cholesky(gram_sum)
    r_factor = jnp.transpose(lower_factor, (0, 2, 1)) / math.sqrt(TOKENS)
    solved = jax.scipy.linalg.solve_triangular(lower_factor, jnp.transpose(blocks, (1, 2, 0)), lower=True)
    whitened = jnp.transpose(solved, (2, 0, 1)).reshape(TOKENS, WIDTH) * math.sqrt(TOKENS)
    return (attn_out, r_factor, whitened)

def reference(queries, keys, values, residual, norm_gain, block_pos, doc_offset):
    outputs = []
    factors = []
    whites = []
    kv_width = KVH * HD
    for copy in range(COPIES):
        attn_part, factor_part, white_part = one_sequence(queries[:, copy * WIDTH:(copy + 1) * WIDTH], keys[:, copy * kv_width:(copy + 1) * kv_width], values[:, copy * kv_width:(copy + 1) * kv_width], residual[:, copy * WIDTH:(copy + 1) * WIDTH], norm_gain, block_pos[copy], doc_offset[copy])
        outputs.append(attn_part)
        factors.append(factor_part)
        whites.append(white_part)
    return (jnp.concatenate(outputs, axis=1), jnp.concatenate(factors, axis=0), jnp.concatenate(whites, axis=1))
```

```python
import functools
import math

import jax
import jax.numpy as jnp
from jax import lax
from jax.experimental import pallas as pl
from jax.experimental.pallas import tpu as pltpu
from jax.sharding import PartitionSpec as P

HEADS = 64
KVH = 8
HD = 128
BLOCK = 128
COPIES = 1
WIDTH = 8192


EPSILON = 1e-05


def positions_and_docs(block_pos, doc_offset):
    block_total = block_pos.shape[0]
    doc_flags = (doc_offset < BLOCK).astype(jnp.int32)
    places = jnp.arange(block_total, dtype=jnp.int32)
    earlier = places[:, None] < places[None, :]
    starts_before = jnp.sum(jnp.where(earlier, doc_flags[:, None], 0), axis=0)
    matches = block_pos[:, None] == jnp.arange(block_total, dtype=jnp.int32)[None, :]
    start_count = jnp.sum(jnp.where(matches, starts_before[None, :], 0), axis=1)
    offsets = jnp.sum(jnp.where(matches, doc_offset[None, :], 0), axis=1)
    within = jnp.arange(BLOCK, dtype=jnp.int32)
    seq_pos = (block_pos[:, None] * BLOCK + within[None, :]).reshape(-1)
    doc_id = (
        start_count[:, None] + (within[None, :] >= offsets[:, None]).astype(jnp.int32)
    ).reshape(-1)
    return (seq_pos, doc_id)


HIGHEST = lax.Precision.HIGHEST
MESH = pl.DeviceIdType.MESH
PANEL = 16
LOG2E = 1.4426950408889634


def iota(shape, dimension):
    return lax.broadcasted_iota(jnp.int32, shape, dimension)


def factor(m_ref):
    count = m_ref.shape[0]
    lane = iota((PANEL, HD), 1)
    sub = iota((PANEL, HD), 0)

    def panel(j, carry):
        base = pl.multiple_of(j * PANEL, PANEL)
        rows = pl.ds(base, PANEL)
        left = [m_ref[c, rows, :HD] for c in range(count)]
        right = [m_ref[c, rows, HD:] for c in range(count)]
        columns = [
            [
                jnp.broadcast_to(
                    jnp.sum(jnp.where(lane == base + i, left[c], 0.0), axis=1, keepdims=True),
                    (PANEL, HD),
                )
                for i in range(PANEL)
            ]
            for c in range(count)
        ]
        scale = [jnp.ones((PANEL, HD), jnp.float32) for c in range(count)]
        for i in range(PANEL):
            for c in range(count):
                pivot = columns[c][i][i : i + 1, :]
                scale[c] = jnp.where(sub == i, lax.rsqrt(pivot), scale[c])
                ratio = jnp.where(sub > i, columns[c][i] * (1.0 / pivot), 0.0)
                left[c] = left[c] - ratio * left[c][i : i + 1, :]
                right[c] = right[c] - ratio * right[c][i : i + 1, :]
                for k in range(i + 1, PANEL):
                    columns[c][k] = columns[c][k] - ratio * columns[c][k][i : i + 1, :]
        for c in range(count):
            both = jnp.concatenate([left[c] * scale[c], right[c] * scale[c]], axis=1)
            m_ref[c, rows, :] = both
            later = jnp.where(lane >= base + PANEL, both[:, :HD], 0.0)
            m_ref[c] = m_ref[c] - lax.dot_general(
                later,
                both,
                (((0,), (0,)), ((), ())),
                precision=HIGHEST,
                preferred_element_type=jnp.float32,
            )
        return carry

    lax.fori_loop(0, HD // PANEL, panel, 0)


def pack(m):
    return jnp.where(iota((HD, HD), 1) >= iota((HD, HD), 0), m[:, :HD], m[:, HD:])


def unpack(x):
    row, col = iota((HD, HD), 0), iota((HD, HD), 1)
    upper = jnp.where(col >= row, x, 0.0)
    inverse = jnp.where(col < row, x, jnp.where(col == row, 1.0 / x, 0.0))
    return (upper, inverse)


def identity():
    return jnp.where(iota((HD, HD), 0) == iota((HD, HD), 1), 1.0, 0.0)


def factor_kernel(g_ref, x_ref, m_ref):
    m_ref[0, :, :HD] = g_ref[0]
    m_ref[0, :, HD:] = identity()
    factor(m_ref)
    x_ref[0] = pack(m_ref[0])


def factor_heads(gram):
    spec = pl.BlockSpec((1, HD, HD), lambda h: (h, 0, 0))
    return pl.pallas_call(
        factor_kernel,
        grid=(gram.shape[0],),
        in_specs=[spec],
        out_specs=spec,
        out_shape=jax.ShapeDtypeStruct(gram.shape, jnp.float32),
        scratch_shapes=[pltpu.VMEM((1, HD, 2 * HD), jnp.float32)],
        name="factor_heads",
    )(gram)


def gram_of(matrix):
    return jnp.einsum("hnc,hnd->hcd", matrix, matrix, precision=lax.Precision.HIGHEST)


def local_generic(queries, keys, values, residual, norm_gain, block_pos, doc_offset):
    row_count = queries.shape[0]
    head_count = queries.shape[1] // HD
    group_size = HEADS // KVH
    share_count = max(1, head_count // group_size)
    per_share = head_count // share_count
    total_rows = row_count * lax.axis_size("seq")
    global_first = lax.axis_index("head") * head_count
    copy_index = global_first // HEADS
    first_head = global_first % HEADS
    first_share = first_head // group_size
    key_start = copy_index * (KVH * HD) + first_share * HD
    key_cols = lax.dynamic_slice_in_dim(keys, key_start, share_count * HD, 1)
    value_cols = lax.dynamic_slice_in_dim(values, key_start, share_count * HD, 1)
    own_blocks = lax.dynamic_index_in_dim(block_pos, copy_index, 0, keepdims=False)
    own_offsets = lax.dynamic_index_in_dim(doc_offset, copy_index, 0, keepdims=False)
    gain_cols = lax.dynamic_slice_in_dim(norm_gain, first_head * HD, head_count * HD)
    seq_pos, doc_id = positions_and_docs(own_blocks, own_offsets)
    first_row = lax.axis_index("seq") * row_count
    own_pos = lax.dynamic_slice_in_dim(seq_pos, first_row, row_count)
    own_doc = lax.dynamic_slice_in_dim(doc_id, first_row, row_count)
    query_heads = queries.reshape(row_count, share_count, per_share, HD)
    score_scale = 1.0 / math.sqrt(HD)

    def attend_block(state_now, key_piece, value_piece, first_key):
        length = key_piece.shape[0]
        key_pos = lax.dynamic_slice_in_dim(seq_pos, first_key, length)
        key_doc = lax.dynamic_slice_in_dim(doc_id, first_key, length)
        seen = (key_pos[None, :] <= own_pos[:, None]) & (key_doc[None, :] == own_doc[:, None])

        def accumulate(state_inner):
            run_max, run_total, run_acc = state_inner
            key_heads = key_piece.reshape(length, share_count, HD)
            value_heads = value_piece.reshape(length, share_count, HD)
            scores = (
                jnp.einsum(
                    "rkgd,nkd->kgrn", query_heads, key_heads, preferred_element_type=jnp.float32
                )
                * score_scale
            )
            scores = jnp.where(seen[None, None], scores, -jnp.inf)
            new_max = jnp.maximum(run_max, jnp.max(scores, axis=3))
            factor = jnp.exp(run_max - new_max)
            expo = jnp.exp(scores - new_max[..., None])
            new_total = run_total * factor + jnp.sum(expo, axis=3)
            partial_value = jnp.einsum(
                "kgrn,nkd->kgrd",
                expo.astype(jnp.bfloat16),
                value_heads,
                preferred_element_type=jnp.float32,
            )
            new_acc = run_acc * factor[..., None] + partial_value
            return (new_max, new_total, new_acc)

        def unchanged(state_inner):
            return state_inner

        return lax.cond(jnp.any(seen), accumulate, unchanged, state_now)

    def attend(state_now, pieces, first_key):
        key_piece, value_piece = pieces
        length = key_piece.shape[0]
        step_rows = math.gcd(length, 1024)
        if step_rows == length:
            return attend_block(state_now, key_piece, value_piece, first_key)

        def advance(step_index, state_inner):
            begin_row = step_index * step_rows
            key_part = lax.dynamic_slice_in_dim(key_piece, begin_row, step_rows, 0)
            value_part = lax.dynamic_slice_in_dim(value_piece, begin_row, step_rows, 0)
            return attend_block(state_inner, key_part, value_part, first_key + begin_row)

        return lax.fori_loop(0, length // step_rows, advance, state_now)

    start_state = (
        jnp.full((share_count, per_share, row_count), -1e30, jnp.float32),
        jnp.zeros((share_count, per_share, row_count), jnp.float32),
        jnp.zeros((share_count, per_share, row_count, HD), jnp.float32),
    )
    final_max, final_total, final_acc = attend(
        start_state,
        (
            lax.all_gather(key_cols, "seq", axis=0, tiled=True),
            lax.all_gather(value_cols, "seq", axis=0, tiled=True),
        ),
        jnp.int32(0),
    )
    output = final_acc / final_total[..., None]
    attn_out = (
        jnp.transpose(output, (2, 0, 1, 3)).reshape(row_count, head_count * HD).astype(jnp.bfloat16)
    )
    mixed = attn_out.astype(jnp.float32) + residual.astype(jnp.float32)
    local_squares = jnp.sum(mixed * mixed, axis=1)
    slot_mask = jnp.arange(COPIES, dtype=jnp.int32) == copy_index
    slotted = jnp.where(slot_mask[:, None], local_squares[None, :], 0.0)
    summed = lax.psum(slotted, "head")
    square_sum = lax.dynamic_index_in_dim(summed, copy_index, 0, keepdims=False)
    normed = mixed * lax.rsqrt(square_sum[:, None] / WIDTH + EPSILON) * gain_cols[None, :]
    blocks = normed.reshape(row_count, head_count, HD)
    head_rows = jnp.transpose(blocks, (1, 0, 2))
    gram_sum = lax.psum(gram_of(head_rows), "seq")
    upper, inverse = unpack(factor_heads(gram_sum))
    r_factor = upper / math.sqrt(total_rows)
    whitened = jnp.einsum("rhc,hdc->rhd", blocks, inverse, precision=HIGHEST)
    whitened = whitened.reshape(row_count, head_count * HD) * math.sqrt(total_rows)
    return (attn_out, r_factor, whitened)


PEERS = 8


def fused_kernel(
    heads,
    head_parts,
    q_ref,
    k_ref,
    v_ref,
    res_ref,
    gain_ref,
    pos_ref,
    off_ref,
    attn_hbm,
    r_hbm,
    white_hbm,
    q_buf,
    res_buf,
    k_buf,
    v_buf,
    bias,
    attn_buf,
    mixed,
    squares,
    g_send,
    g_recv,
    m_ref,
    x_buf,
    r_buf,
    white_buf,
    local_sem,
    kv_send,
    kv_recv,
    sq_send,
    sq_recv,
    g_send_sem,
    g_recv_sem,
    x_send,
    x_recv,
):
    me = lax.axis_index("seq")
    part = lax.axis_index("head")
    group = HEADS // KVH
    shares = heads // group
    width = shares * HD
    core = me % 2
    bit_x = (me // 2) % 2
    bit_y = me // 4
    to_sib = 1 - 2 * core
    to_x = 2 - 4 * bit_x
    to_y = 4 - 8 * bit_y
    sib = me + to_sib
    near = [me + to_x + to_y, me + to_x, me + to_y]

    key_cols = pl.ds(pl.multiple_of(part * width, HD), width)
    own_rows = pl.ds(pl.multiple_of(me * BLOCK, BLOCK), BLOCK)
    loads = [
        pltpu.make_async_copy(k_ref.at[:, key_cols], k_buf.at[own_rows], local_sem.at[0]),
        pltpu.make_async_copy(v_ref.at[:, key_cols], v_buf.at[own_rows], local_sem.at[1]),
        pltpu.make_async_copy(q_ref, q_buf, local_sem.at[2]),
        pltpu.make_async_copy(res_ref, res_buf, local_sem.at[3]),
    ]
    for copy in loads:
        copy.start()

    barrier = pltpu.get_barrier_semaphore()
    for step in range(1, PEERS):
        pl.semaphore_signal(
            barrier, inc=1, device_id=((me + step) % PEERS, part), device_id_type=MESH
        )
    for step in range(1, head_parts):
        pl.semaphore_signal(
            barrier, inc=1, device_id=(me, (part + step) % head_parts), device_id_type=MESH
        )
    pl.semaphore_wait(barrier, PEERS - 1 + head_parts - 1)

    def remote(src, dst, send, recv, device):
        return pltpu.make_async_remote_copy(
            src_ref=src,
            dst_ref=dst,
            send_sem=send,
            recv_sem=recv,
            device_id=device,
            device_id_type=MESH,
        )

    def spread(slot_of, send, recv):
        copies = []
        for t, peer in enumerate(near + [sib]):
            copy = remote(slot_of(me), slot_of(me), send.at[t], recv.at[me], (peer, part))
            copy.start()
            copies.append(copy)
        return copies

    def arrived(slot_of, send, recv, owner):
        remote(slot_of(owner), slot_of(owner), send.at[0], recv.at[owner], (sib, part)).wait_recv()

    def forward(slot_of, send, recv, t):
        owner = near[t]
        arrived(slot_of, send, recv, owner)
        copy = remote(slot_of(owner), slot_of(owner), send.at[4 + t], recv.at[owner], (sib, part))
        copy.start()
        return copy

    def rows_of(buf):
        return lambda owner: buf.at[pl.ds(pl.multiple_of(owner * BLOCK, BLOCK), BLOCK)]

    pending = []
    kv = [(rows_of(k_buf), kv_send.at[0], kv_recv.at[0]), (rows_of(v_buf), kv_send.at[1], kv_recv.at[1])]
    for i, way in enumerate(kv):
        loads[i].wait()
        pending += spread(*way)

    row_pos = pos_ref[0, me]
    lane = iota((BLOCK, BLOCK), 1)
    sub = iota((BLOCK, BLOCK), 0)

    def starts(position):
        total = jnp.int32(0)
        for b in range(PEERS):
            counted = (b < position) & (off_ref[0, b] < BLOCK)
            total = total + jnp.where(counted, 1, 0)
        return total

    own_pos = row_pos * BLOCK + sub
    own_doc = starts(row_pos) + jnp.where(sub >= off_ref[0, row_pos], 1, 0)
    for s in range(PEERS):
        position = pos_ref[0, s]
        key_pos = position * BLOCK + lane
        key_doc = starts(position) + jnp.where(lane >= off_ref[0, position], 1, 0)
        seen = (key_pos <= own_pos) & (key_doc == own_doc)
        bias[:, s * BLOCK : (s + 1) * BLOCK] = jnp.where(seen, 0.0, -jnp.inf)

    for t in range(3):
        for way in kv:
            pending.append(forward(*way, t))
    for owner in [sib] + [peer + to_sib for peer in near]:
        for way in kv:
            arrived(*way, owner)
    loads[2].wait()
    loads[3].wait()

    def attend(h, square):
        cols = pl.ds(pl.multiple_of(h * HD, HD), HD)
        share = pl.ds(pl.multiple_of((h // group) * HD, HD), HD)
        scores = lax.dot_general(
            q_buf[:, cols],
            k_buf[:, share],
            (((1,), (1,)), ((), ())),
            preferred_element_type=jnp.float32,
        )
        scores = scores + bias[...]
        top = jnp.max(scores, axis=1, keepdims=True)
        expo = jnp.exp2((scores - top) * (LOG2E / math.sqrt(HD)))
        total = jnp.sum(expo, axis=1, keepdims=True)
        out = lax.dot_general(
            expo.astype(jnp.bfloat16),
            v_buf[:, share],
            (((1,), (0,)), ((), ())),
            preferred_element_type=jnp.float32,
        )
        out = (out / total).astype(jnp.bfloat16)
        attn_buf[:, cols] = out
        mix = out.astype(jnp.float32) + res_buf[:, cols].astype(jnp.float32)
        mixed[:, cols] = mix
        return square + mix * mix

    square = lax.fori_loop(
        0, heads, attend, jnp.zeros((BLOCK, HD), jnp.float32), unroll=4
    )
    attn_out = pltpu.make_async_copy(attn_buf, attn_hbm, local_sem.at[4])
    attn_out.start()

    squares[part] = jnp.broadcast_to(jnp.sum(square.T, axis=0, keepdims=True), (8, HD))
    for step in range(1, head_parts):
        copy = remote(
            squares.at[part],
            squares.at[part],
            sq_send.at[step],
            sq_recv.at[part],
            (me, (part + step) % head_parts),
        )
        copy.start()
        pending.append(copy)
    for step in range(1, head_parts):
        other = (part + step) % head_parts
        remote(
            squares.at[other], squares.at[other], sq_send.at[step], sq_recv.at[other], (me, other)
        ).wait_recv()
    total = squares[0]
    for p in range(1, head_parts):
        total = total + squares[p]
    inv_rms = lax.rsqrt(total[0:1, :] / WIDTH + EPSILON)
    inv_rms = jnp.broadcast_to(inv_rms, (BLOCK, HD)).T

    def gram(h):
        cols = pl.ds(pl.multiple_of(h * HD, HD), HD)
        normed = mixed[:, cols] * inv_rms * gain_ref[pl.ds(part * heads + h, 1), :]
        mixed[:, cols] = normed
        return lax.dot_general(
            normed,
            normed,
            (((0,), (0,)), ((), ())),
            precision=HIGHEST,
            preferred_element_type=jnp.float32,
        )

    def make_pair(p, ref):
        first, second = gram(2 * p), gram(2 * p + 1)
        ref[:HD, :] = jnp.where(sub >= lane, first, second)
        diagonal = jnp.sum(jnp.where(sub == lane, second, 0.0), axis=0, keepdims=True)
        ref[HD:, :] = jnp.broadcast_to(diagonal, (8, HD))

    def send_pair(step):
        peer = (me + step) % PEERS
        return remote(
            g_send.at[peer], g_recv.at[me], g_send_sem.at[step], g_recv_sem.at[me], (peer, part)
        )

    def make_and_send(step, carry):
        peer = (me + step) % PEERS
        make_pair(peer, g_send.at[peer])
        send_pair(step).start()
        return carry

    lax.fori_loop(1, PEERS, make_and_send, 0)
    make_pair(me, g_recv.at[me])
    for step in range(1, PEERS):
        source = (me + step) % PEERS
        remote(
            g_recv.at[source], g_recv.at[source], g_send_sem.at[step], g_recv_sem.at[source], (source, part)
        ).wait_recv()
    gram_sum = g_recv[0]
    for s in range(1, PEERS):
        gram_sum = gram_sum + g_recv[s]
    body = gram_sum[:HD, :]
    turned = body.T
    eye = sub == lane
    m_ref[0, :, :HD] = jnp.where(sub >= lane, body, turned)
    m_ref[1, :, :HD] = jnp.where(
        eye, gram_sum[HD : HD + 1, :], jnp.where(sub < lane, body, turned)
    )
    for c in range(2):
        m_ref[c, :, HD:] = identity()
    factor(m_ref)
    for c in range(2):
        x_buf[me, c] = pack(m_ref[c])

    slot = (lambda owner: x_buf.at[owner], x_send, x_recv)
    pending += spread(*slot)
    root = math.sqrt(BLOCK * PEERS)

    def finish(owner):
        for c in range(2):
            h = 2 * owner + c
            cols = pl.ds(pl.multiple_of(h * HD, HD), HD)
            upper, inverse = unpack(x_buf[owner, c])
            r_buf[h] = upper * (1.0 / root)
            white_buf[:, cols] = root * lax.dot_general(
                mixed[:, cols],
                inverse,
                (((1,), (1,)), ((), ())),
                precision=HIGHEST,
                preferred_element_type=jnp.float32,
            )

    finish(me)
    arrived(*slot, sib)
    finish(sib)
    for t in (1, 2, 0):
        pending.append(forward(*slot, t))
        finish(near[t])
    for t in (1, 2, 0):
        arrived(*slot, near[t] + to_sib)
        finish(near[t] + to_sib)

    outs = [
        pltpu.make_async_copy(r_buf, r_hbm, local_sem.at[5]),
        pltpu.make_async_copy(white_buf, white_hbm, local_sem.at[6]),
    ]
    for copy in outs:
        copy.start()
    for copy in pending:
        copy.wait_send()
    for step in range(1, PEERS):
        send_pair(step).wait_send()
    attn_out.wait()
    for copy in outs:
        copy.wait()


def local_fused(head_parts, queries, keys, values, residual, norm_gain, block_pos, doc_offset):
    rows, columns = queries.shape
    heads = columns // HD
    width = heads // (HEADS // KVH) * HD
    f32, bf16 = jnp.float32, jnp.bfloat16
    anywhere = pl.BlockSpec(memory_space=pl.ANY)
    scalars = pl.BlockSpec(memory_space=pltpu.SMEM)
    dma = pltpu.SemaphoreType.DMA
    return pl.pallas_call(
        functools.partial(fused_kernel, heads, head_parts),
        in_specs=[anywhere] * 4 + [pl.BlockSpec(memory_space=pltpu.VMEM), scalars, scalars],
        out_specs=(anywhere,) * 3,
        out_shape=(
            jax.ShapeDtypeStruct((rows, columns), bf16),
            jax.ShapeDtypeStruct((heads, HD, HD), f32),
            jax.ShapeDtypeStruct((rows, columns), f32),
        ),
        scratch_shapes=[
            pltpu.VMEM((rows, columns), bf16),
            pltpu.VMEM((rows, columns), bf16),
            pltpu.VMEM((PEERS * BLOCK, width), bf16),
            pltpu.VMEM((PEERS * BLOCK, width), bf16),
            pltpu.VMEM((BLOCK, PEERS * BLOCK), f32),
            pltpu.VMEM((rows, columns), bf16),
            pltpu.VMEM((rows, columns), f32),
            pltpu.VMEM((head_parts, 8, HD), f32),
            pltpu.VMEM((PEERS, HD + 8, HD), f32),
            pltpu.VMEM((PEERS, HD + 8, HD), f32),
            pltpu.VMEM((2, HD, 2 * HD), f32),
            pltpu.VMEM((PEERS, 2, HD, HD), f32),
            pltpu.VMEM((heads, HD, HD), f32),
            pltpu.VMEM((rows, columns), f32),
            dma((7,)),
            dma((2, 7)),
            dma((2, PEERS)),
            dma((head_parts,)),
            dma((head_parts,)),
            dma((PEERS,)),
            dma((PEERS,)),
            dma((7,)),
            dma((PEERS,)),
        ],
        compiler_params=pltpu.CompilerParams(
            collective_id=0, has_side_effects=True, vmem_limit_bytes=40 * 2**20
        ),
        name="fused",
    )(queries, keys, values, residual, norm_gain.reshape(HEADS, HD), block_pos, doc_offset)


def solution(mesh):
    peers, head_parts = mesh.shape["seq"], mesh.shape["head"]
    if peers == PEERS and HEADS // head_parts == 2 * PEERS:
        local = functools.partial(local_fused, head_parts)
    else:
        local = local_generic
    return jax.shard_map(
        local,
        mesh=mesh,
        in_specs=(
            P("seq", "head"),
            P("seq", None),
            P("seq", None),
            P("seq", "head"),
            P(),
            P(),
            P(),
        ),
        out_specs=(P("seq", "head"), P("head", None, None), P("seq", "head")),
        check_vma=False,
    )
```

```python
import functools
import math

import jax
import jax.numpy as jnp
from jax import lax
from jax.experimental import pallas as pl
from jax.experimental.pallas import tpu as pltpu
from jax.sharding import PartitionSpec as P

HEADS = 64
KVH = 8
HD = 128
BLOCK = 128
COPIES = 1
WIDTH = 8192


EPSILON = 1e-05


def positions_and_docs(block_pos, doc_offset):
    block_total = block_pos.shape[0]
    doc_flags = (doc_offset < BLOCK).astype(jnp.int32)
    places = jnp.arange(block_total, dtype=jnp.int32)
    earlier = places[:, None] < places[None, :]
    starts_before = jnp.sum(jnp.where(earlier, doc_flags[:, None], 0), axis=0)
    matches = block_pos[:, None] == jnp.arange(block_total, dtype=jnp.int32)[None, :]
    start_count = jnp.sum(jnp.where(matches, starts_before[None, :], 0), axis=1)
    offsets = jnp.sum(jnp.where(matches, doc_offset[None, :], 0), axis=1)
    within = jnp.arange(BLOCK, dtype=jnp.int32)
    seq_pos = (block_pos[:, None] * BLOCK + within[None, :]).reshape(-1)
    doc_id = (
        start_count[:, None] + (within[None, :] >= offsets[:, None]).astype(jnp.int32)
    ).reshape(-1)
    return (seq_pos, doc_id)


HIGHEST = lax.Precision.HIGHEST
MESH = pl.DeviceIdType.MESH
PANEL = 16
LOG2E = 1.4426950408889634


def iota(shape, dimension):
    return lax.broadcasted_iota(jnp.int32, shape, dimension)


def factor(m_ref):
    count = m_ref.shape[0]
    lane = iota((PANEL, HD), 1)
    sub = iota((PANEL, HD), 0)

    def panel(j, carry):
        base = pl.multiple_of(j * PANEL, PANEL)
        rows = pl.ds(base, PANEL)
        left = [m_ref[c, rows, :HD] for c in range(count)]
        right = [m_ref[c, rows, HD:] for c in range(count)]
        columns = [
            [
                jnp.broadcast_to(
                    jnp.sum(jnp.where(lane == base + i, left[c], 0.0), axis=1, keepdims=True),
                    (PANEL, HD),
                )
                for i in range(PANEL)
            ]
            for c in range(count)
        ]
        scale = [jnp.ones((PANEL, HD), jnp.float32) for c in range(count)]
        for i in range(PANEL):
            for c in range(count):
                pivot = columns[c][i][i : i + 1, :]
                scale[c] = jnp.where(sub == i, lax.rsqrt(pivot), scale[c])
                ratio = jnp.where(sub > i, columns[c][i] * (1.0 / pivot), 0.0)
                left[c] = left[c] - ratio * left[c][i : i + 1, :]
                right[c] = right[c] - ratio * right[c][i : i + 1, :]
                for k in range(i + 1, PANEL):
                    columns[c][k] = columns[c][k] - ratio * columns[c][k][i : i + 1, :]
        for c in range(count):
            both = jnp.concatenate([left[c] * scale[c], right[c] * scale[c]], axis=1)
            m_ref[c, rows, :] = both
            later = jnp.where(lane >= base + PANEL, both[:, :HD], 0.0)
            m_ref[c] = m_ref[c] - lax.dot_general(
                later,
                both,
                (((0,), (0,)), ((), ())),
                precision=HIGHEST,
                preferred_element_type=jnp.float32,
            )
        return carry

    lax.fori_loop(0, HD // PANEL, panel, 0)


def pack(m):
    return jnp.where(iota((HD, HD), 1) >= iota((HD, HD), 0), m[:, :HD], m[:, HD:])


def unpack(x):
    row, col = iota((HD, HD), 0), iota((HD, HD), 1)
    upper = jnp.where(col >= row, x, 0.0)
    inverse = jnp.where(col < row, x, jnp.where(col == row, 1.0 / x, 0.0))
    return (upper, inverse)


def identity():
    return jnp.where(iota((HD, HD), 0) == iota((HD, HD), 1), 1.0, 0.0)


def factor_kernel(g_ref, x_ref, m_ref):
    m_ref[0, :, :HD] = g_ref[0]
    m_ref[0, :, HD:] = identity()
    factor(m_ref)
    x_ref[0] = pack(m_ref[0])


def factor_heads(gram):
    spec = pl.BlockSpec((1, HD, HD), lambda h: (h, 0, 0))
    return pl.pallas_call(
        factor_kernel,
        grid=(gram.shape[0],),
        in_specs=[spec],
        out_specs=spec,
        out_shape=jax.ShapeDtypeStruct(gram.shape, jnp.float32),
        scratch_shapes=[pltpu.VMEM((1, HD, 2 * HD), jnp.float32)],
        name="factor_heads",
    )(gram)


def gram_of(matrix):
    return jnp.einsum("hnc,hnd->hcd", matrix, matrix, precision=lax.Precision.HIGHEST)


def local_generic(queries, keys, values, residual, norm_gain, block_pos, doc_offset):
    row_count = queries.shape[0]
    head_count = queries.shape[1] // HD
    group_size = HEADS // KVH
    share_count = max(1, head_count // group_size)
    per_share = head_count // share_count
    total_rows = row_count * lax.axis_size("seq")
    global_first = lax.axis_index("head") * head_count
    copy_index = global_first // HEADS
    first_head = global_first % HEADS
    first_share = first_head // group_size
    key_start = copy_index * (KVH * HD) + first_share * HD
    key_cols = lax.dynamic_slice_in_dim(keys, key_start, share_count * HD, 1)
    value_cols = lax.dynamic_slice_in_dim(values, key_start, share_count * HD, 1)
    own_blocks = lax.dynamic_index_in_dim(block_pos, copy_index, 0, keepdims=False)
    own_offsets = lax.dynamic_index_in_dim(doc_offset, copy_index, 0, keepdims=False)
    gain_cols = lax.dynamic_slice_in_dim(norm_gain, first_head * HD, head_count * HD)
    seq_pos, doc_id = positions_and_docs(own_blocks, own_offsets)
    first_row = lax.axis_index("seq") * row_count
    own_pos = lax.dynamic_slice_in_dim(seq_pos, first_row, row_count)
    own_doc = lax.dynamic_slice_in_dim(doc_id, first_row, row_count)
    query_heads = queries.reshape(row_count, share_count, per_share, HD)
    score_scale = 1.0 / math.sqrt(HD)

    def attend_block(state_now, key_piece, value_piece, first_key):
        length = key_piece.shape[0]
        key_pos = lax.dynamic_slice_in_dim(seq_pos, first_key, length)
        key_doc = lax.dynamic_slice_in_dim(doc_id, first_key, length)
        seen = (key_pos[None, :] <= own_pos[:, None]) & (key_doc[None, :] == own_doc[:, None])

        def accumulate(state_inner):
            run_max, run_total, run_acc = state_inner
            key_heads = key_piece.reshape(length, share_count, HD)
            value_heads = value_piece.reshape(length, share_count, HD)
            scores = (
                jnp.einsum(
                    "rkgd,nkd->kgrn", query_heads, key_heads, preferred_element_type=jnp.float32
                )
                * score_scale
            )
            scores = jnp.where(seen[None, None], scores, -jnp.inf)
            new_max = jnp.maximum(run_max, jnp.max(scores, axis=3))
            factor = jnp.exp(run_max - new_max)
            expo = jnp.exp(scores - new_max[..., None])
            new_total = run_total * factor + jnp.sum(expo, axis=3)
            partial_value = jnp.einsum(
                "kgrn,nkd->kgrd",
                expo.astype(jnp.bfloat16),
                value_heads,
                preferred_element_type=jnp.float32,
            )
            new_acc = run_acc * factor[..., None] + partial_value
            return (new_max, new_total, new_acc)

        def unchanged(state_inner):
            return state_inner

        return lax.cond(jnp.any(seen), accumulate, unchanged, state_now)

    def attend(state_now, pieces, first_key):
        key_piece, value_piece = pieces
        length = key_piece.shape[0]
        step_rows = math.gcd(length, 1024)
        if step_rows == length:
            return attend_block(state_now, key_piece, value_piece, first_key)

        def advance(step_index, state_inner):
            begin_row = step_index * step_rows
            key_part = lax.dynamic_slice_in_dim(key_piece, begin_row, step_rows, 0)
            value_part = lax.dynamic_slice_in_dim(value_piece, begin_row, step_rows, 0)
            return attend_block(state_inner, key_part, value_part, first_key + begin_row)

        return lax.fori_loop(0, length // step_rows, advance, state_now)

    start_state = (
        jnp.full((share_count, per_share, row_count), -1e30, jnp.float32),
        jnp.zeros((share_count, per_share, row_count), jnp.float32),
        jnp.zeros((share_count, per_share, row_count, HD), jnp.float32),
    )
    final_max, final_total, final_acc = attend(
        start_state,
        (
            lax.all_gather(key_cols, "seq", axis=0, tiled=True),
            lax.all_gather(value_cols, "seq", axis=0, tiled=True),
        ),
        jnp.int32(0),
    )
    output = final_acc / final_total[..., None]
    attn_out = (
        jnp.transpose(output, (2, 0, 1, 3)).reshape(row_count, head_count * HD).astype(jnp.bfloat16)
    )
    mixed = attn_out.astype(jnp.float32) + residual.astype(jnp.float32)
    local_squares = jnp.sum(mixed * mixed, axis=1)
    slot_mask = jnp.arange(COPIES, dtype=jnp.int32) == copy_index
    slotted = jnp.where(slot_mask[:, None], local_squares[None, :], 0.0)
    summed = lax.psum(slotted, "head")
    square_sum = lax.dynamic_index_in_dim(summed, copy_index, 0, keepdims=False)
    normed = mixed * lax.rsqrt(square_sum[:, None] / WIDTH + EPSILON) * gain_cols[None, :]
    blocks = normed.reshape(row_count, head_count, HD)
    head_rows = jnp.transpose(blocks, (1, 0, 2))
    gram_sum = lax.psum(gram_of(head_rows), "seq")
    upper, inverse = unpack(factor_heads(gram_sum))
    r_factor = upper / math.sqrt(total_rows)
    whitened = jnp.einsum("rhc,hdc->rhd", blocks, inverse, precision=HIGHEST)
    whitened = whitened.reshape(row_count, head_count * HD) * math.sqrt(total_rows)
    return (attn_out, r_factor, whitened)


PEERS = 8


def fused_kernel(
    heads,
    head_parts,
    q_ref,
    k_ref,
    v_ref,
    res_ref,
    gain_hbm,
    pos_hbm,
    off_hbm,
    attn_buf,
    r_buf,
    white_buf,
    q_buf,
    res_buf,
    k_buf,
    v_buf,
    bias,
    mixed,
    squares,
    g_send,
    g_recv,
    g_half,
    m_ref,
    w_buf,
    u_buf,
    gain_ref,
    pos_ref,
    off_ref,
    local_sem,
    kv_send,
    kv_recv,
    sq_send,
    sq_recv,
    g_send_sem,
    g_recv_sem,
    half_send,
    half_recv,
    w_send,
    w_recv,
    u_send,
    u_recv,
):
    me = lax.axis_index("seq")
    part = lax.axis_index("head")
    group = HEADS // KVH
    shares = heads // group
    width = shares * HD
    core = me % 2
    bit_x = (me // 2) % 2
    bit_y = me // 4
    to_sib = 1 - 2 * core
    to_x = 2 - 4 * bit_x
    to_y = 4 - 8 * bit_y
    sib = me + to_sib
    near = [me + to_x + to_y, me + to_x, me + to_y]

    key_cols = pl.ds(pl.multiple_of(part * width, HD), width)
    own_rows = pl.ds(pl.multiple_of(me * BLOCK, BLOCK), BLOCK)
    loads = [
        pltpu.make_async_copy(k_ref.at[:, key_cols], k_buf.at[own_rows], local_sem.at[0]),
        pltpu.make_async_copy(v_ref.at[:, key_cols], v_buf.at[own_rows], local_sem.at[1]),
        pltpu.make_async_copy(q_ref, q_buf, local_sem.at[2]),
        pltpu.make_async_copy(res_ref, res_buf, local_sem.at[3]),
        pltpu.make_async_copy(pos_hbm, pos_ref, local_sem.at[4]),
        pltpu.make_async_copy(off_hbm, off_ref, local_sem.at[5]),
        pltpu.make_async_copy(gain_hbm, gain_ref, local_sem.at[6]),
    ]
    for copy in loads:
        copy.start()

    barrier = pltpu.get_barrier_semaphore()
    for step in range(1, PEERS):
        pl.semaphore_signal(
            barrier, inc=1, device_id=((me + step) % PEERS, part), device_id_type=MESH
        )
    for step in range(1, head_parts):
        pl.semaphore_signal(
            barrier, inc=1, device_id=(me, (part + step) % head_parts), device_id_type=MESH
        )
    pl.semaphore_wait(barrier, PEERS - 1 + head_parts - 1)

    def remote(src, dst, send, recv, device):
        return pltpu.make_async_remote_copy(
            src_ref=src,
            dst_ref=dst,
            send_sem=send,
            recv_sem=recv,
            device_id=device,
            device_id_type=MESH,
        )

    def spread(slot_of, send, recv):
        copies = []
        for t, peer in enumerate(near + [sib]):
            copy = remote(slot_of(me), slot_of(me), send.at[t], recv.at[me], (peer, part))
            copy.start()
            copies.append(copy)
        return copies

    def arrived(slot_of, send, recv, owner):
        remote(slot_of(owner), slot_of(owner), send.at[0], recv.at[owner], (sib, part)).wait_recv()

    def forward(slot_of, send, recv, t):
        owner = near[t]
        arrived(slot_of, send, recv, owner)
        copy = remote(slot_of(owner), slot_of(owner), send.at[4 + t], recv.at[owner], (sib, part))
        copy.start()
        return copy

    def part_of(buf, share):
        cols = slice(share * HD, (share + 1) * HD)
        return lambda owner: buf.at[pl.ds(pl.multiple_of(owner * BLOCK, BLOCK), BLOCK), cols]

    pending = []
    kv = [
        [
            (part_of(buf, share), kv_send.at[share, i], kv_recv.at[share, i])
            for i, buf in enumerate((k_buf, v_buf))
        ]
        for share in range(shares)
    ]
    loads[0].wait()
    loads[1].wait()
    for ways in kv:
        for way in ways:
            pending += spread(*way)

    def pass_on(share, t):
        for way in kv[share]:
            pending.append(forward(*way, t))

    def complete(share):
        for owner in [sib] + [peer + to_sib for peer in near]:
            for way in kv[share]:
                arrived(*way, owner)

    loads[4].wait()
    loads[5].wait()
    row_pos = pos_ref[0, me]
    lane = iota((BLOCK, BLOCK), 1)
    sub = iota((BLOCK, BLOCK), 0)

    def starts(position):
        total = jnp.int32(0)
        for b in range(PEERS):
            counted = (b < position) & (off_ref[0, b] < BLOCK)
            total = total + jnp.where(counted, 1, 0)
        return total

    own_pos = row_pos * BLOCK + sub
    own_doc = starts(row_pos) + jnp.where(sub >= off_ref[0, row_pos], 1, 0)
    for s in range(PEERS):
        position = pos_ref[0, s]
        key_pos = position * BLOCK + lane
        key_doc = starts(position) + jnp.where(lane >= off_ref[0, position], 1, 0)
        seen = (key_pos <= own_pos) & (key_doc == own_doc)
        bias[:, s * BLOCK : (s + 1) * BLOCK] = jnp.where(seen, 0.0, -jnp.inf)

    for t in (1, 2, 0):
        pass_on(0, t)
    complete(0)
    loads[2].wait()
    loads[3].wait()
    loads[6].wait()

    def attend(h, square):
        cols = pl.ds(pl.multiple_of(h * HD, HD), HD)
        share = pl.ds(pl.multiple_of((h // group) * HD, HD), HD)
        scores = lax.dot_general(
            q_buf[:, cols],
            k_buf[:, share],
            (((1,), (1,)), ((), ())),
            preferred_element_type=jnp.float32,
        )
        scores = scores + bias[...]
        top = jnp.max(scores, axis=1, keepdims=True)
        expo = jnp.exp2((scores - top) * (LOG2E / math.sqrt(HD)))
        total = jnp.sum(expo, axis=1, keepdims=True)
        out = lax.dot_general(
            expo.astype(jnp.bfloat16),
            v_buf[:, share],
            (((1,), (0,)), ((), ())),
            preferred_element_type=jnp.float32,
        )
        out = (out / total).astype(jnp.bfloat16)
        attn_buf[:, cols] = out
        mix = out.astype(jnp.float32) + res_buf[:, cols].astype(jnp.float32)
        mixed[:, cols] = mix
        return square + mix * mix

    square = jnp.zeros((BLOCK, HD), jnp.float32)
    for h in range(group // 2):
        square = attend(h, square)
    pass_on(1, 1)
    pass_on(1, 2)
    for h in range(group // 2, group):
        square = attend(h, square)
    pass_on(1, 0)
    complete(1)
    square = lax.fori_loop(group, heads, attend, square, unroll=4)

    squares[part] = jnp.broadcast_to(jnp.sum(square.T, axis=0, keepdims=True), (8, HD))
    for step in range(1, head_parts):
        copy = remote(
            squares.at[part],
            squares.at[part],
            sq_send.at[step],
            sq_recv.at[part],
            (me, (part + step) % head_parts),
        )
        copy.start()
        pending.append(copy)
    for step in range(1, head_parts):
        other = (part + step) % head_parts
        remote(
            squares.at[other], squares.at[other], sq_send.at[step], sq_recv.at[other], (me, other)
        ).wait_recv()
    total = squares[0]
    for p in range(1, head_parts):
        total = total + squares[p]
    inv_rms = lax.rsqrt(total[0:1, :] / WIDTH + EPSILON)
    inv_rms = jnp.broadcast_to(inv_rms, (BLOCK, HD)).T

    def gram(h):
        cols = pl.ds(pl.multiple_of(h * HD, HD), HD)
        normed = mixed[:, cols] * inv_rms * gain_ref[pl.ds(part * heads + h, 1), :]
        mixed[:, cols] = normed
        return lax.dot_general(
            normed,
            normed,
            (((0,), (0,)), ((), ())),
            precision=HIGHEST,
            preferred_element_type=jnp.float32,
        )

    def make_pair(p, ref):
        first, second = gram(2 * p), gram(2 * p + 1)
        ref[:HD, :] = jnp.where(sub >= lane, first, second)
        diagonal = jnp.sum(jnp.where(sub == lane, second, 0.0), axis=0, keepdims=True)
        ref[HD:, :] = jnp.broadcast_to(diagonal, (8, HD))

    chip = me // 2
    chips = PEERS // 2
    for k in range(1, chips + 1):
        target = (chip + k) % chips
        make_pair(2 * target + 1 - core, g_send.at[target])
        copy = remote(
            g_send.at[target], g_half.at[target], half_send.at[k - 1], half_recv.at[target], (sib, part)
        )
        copy.start()
        pending.append(copy)

    def half(target):
        remote(
            g_half.at[target], g_half.at[target], half_send.at[0], half_recv.at[target], (sib, part)
        ).wait_recv()
        return g_half[target]

    for k in range(1, chips):
        target = (chip + k) % chips
        slot = g_send.at[chips + target]
        make_pair(2 * target + core, slot)
        slot[...] = slot[...] + half(target)
        copy = remote(
            slot, g_recv.at[chip], g_send_sem.at[k], g_recv_sem.at[chip], (2 * target + core, part)
        )
        copy.start()
        pending.append(copy)
    make_pair(me, g_recv.at[chip])
    g_recv[chip] = g_recv[chip] + half(chip)
    for k in range(1, chips):
        source = (chip + k) % chips
        remote(
            g_recv.at[source],
            g_recv.at[source],
            g_send_sem.at[k],
            g_recv_sem.at[source],
            (2 * source + core, part),
        ).wait_recv()
    gram_sum = g_recv[0]
    for c in range(1, chips):
        gram_sum = gram_sum + g_recv[c]
    body = gram_sum[:HD, :]
    turned = body.T
    eye = sub == lane
    m_ref[0, :, :HD] = jnp.where(sub >= lane, body, turned)
    m_ref[1, :, :HD] = jnp.where(
        eye, gram_sum[HD : HD + 1, :], jnp.where(sub < lane, body, turned)
    )
    for c in range(2):
        m_ref[c, :, HD:] = identity()
    factor(m_ref)
    root = math.sqrt(BLOCK * PEERS)

    second = m_ref[1, :, HD:]
    diagonal = jnp.sum(jnp.where(eye, second, 0.0), axis=0, keepdims=True)
    w_buf[me, :HD, :] = jnp.where(sub >= lane, m_ref[0, :, HD:], second.T)
    w_buf[me, HD:, :] = jnp.broadcast_to(diagonal, (8, HD))
    w_way = (lambda owner: w_buf.at[owner], w_send, w_recv)
    pending += spread(*w_way)
    second = m_ref[1, :, :HD]
    diagonal = jnp.sum(jnp.where(eye, second, 0.0), axis=0, keepdims=True)
    pair = jnp.where(sub <= lane, m_ref[0, :, :HD], second.T)
    u_buf[me, :HD, :] = (pair * (1.0 / root)).astype(jnp.bfloat16)
    u_buf[me, HD:, :] = jnp.broadcast_to(diagonal * (1.0 / root), (16, HD)).astype(jnp.bfloat16)
    u_way = (lambda owner: u_buf.at[owner], u_send, u_recv)
    pending += spread(*u_way)

    def whiten(owner):
        body = w_buf[owner, :HD, :]
        diagonal = w_buf[owner, HD : HD + 1, :]
        first = jnp.where(sub >= lane, body, 0.0)
        second = jnp.where(sub < lane, body, jnp.where(eye, diagonal, 0.0))
        for c, (inverse, side) in enumerate(((first, 1), (second, 0))):
            cols = pl.ds(pl.multiple_of((2 * owner + c) * HD, HD), HD)
            white_buf[:, cols] = root * lax.dot_general(
                mixed[:, cols],
                inverse,
                (((1,), (side,)), ((), ())),
                precision=HIGHEST,
                preferred_element_type=jnp.float32,
            )

    def expand(owner):
        body = u_buf[owner, :HD, :].astype(jnp.float32)
        diagonal = u_buf[owner, HD:, :].astype(jnp.float32)[0:1, :]
        r_buf[2 * owner] = jnp.where(sub <= lane, body, 0.0)
        r_buf[2 * owner + 1] = jnp.where(sub < lane, body.T, jnp.where(eye, diagonal, 0.0))

    whiten(me)
    arrived(*w_way, sib)
    whiten(sib)
    for t in (1, 2, 0):
        pending.append(forward(*w_way, t))
        whiten(near[t])
    expand(me)
    arrived(*u_way, sib)
    expand(sib)
    for t in (1, 2, 0):
        pending.append(forward(*u_way, t))
        arrived(*w_way, near[t] + to_sib)
        whiten(near[t] + to_sib)
        expand(near[t])
    for t in (1, 2, 0):
        arrived(*u_way, near[t] + to_sib)
        expand(near[t] + to_sib)
    for copy in pending:
        copy.wait_send()


def local_fused(head_parts, queries, keys, values, residual, norm_gain, block_pos, doc_offset):
    rows, columns = queries.shape
    heads = columns // HD
    width = heads // (HEADS // KVH) * HD
    f32, bf16 = jnp.float32, jnp.bfloat16
    outside = pl.BlockSpec(memory_space=pltpu.HBM)
    inside = pl.BlockSpec(memory_space=pltpu.VMEM)
    dma = pltpu.SemaphoreType.DMA
    return pl.pallas_call(
        functools.partial(fused_kernel, heads, head_parts),
        in_specs=[outside] * 7,
        out_specs=(inside,) * 3,
        out_shape=(
            jax.ShapeDtypeStruct((rows, columns), bf16),
            jax.ShapeDtypeStruct((heads, HD, HD), f32),
            jax.ShapeDtypeStruct((rows, columns), f32),
        ),
        scratch_shapes=[
            pltpu.VMEM((rows, columns), bf16),
            pltpu.VMEM((rows, columns), bf16),
            pltpu.VMEM((PEERS * BLOCK, width), bf16),
            pltpu.VMEM((PEERS * BLOCK, width), bf16),
            pltpu.VMEM((BLOCK, PEERS * BLOCK), f32),
            pltpu.VMEM((rows, columns), f32),
            pltpu.VMEM((head_parts, 8, HD), f32),
            pltpu.VMEM((PEERS, HD + 8, HD), f32),
            pltpu.VMEM((PEERS // 2, HD + 8, HD), f32),
            pltpu.VMEM((PEERS // 2, HD + 8, HD), f32),
            pltpu.VMEM((2, HD, 2 * HD), f32),
            pltpu.VMEM((PEERS, HD + 8, HD), f32),
            pltpu.VMEM((PEERS, HD + 16, HD), bf16),
            pltpu.VMEM((HEADS, HD), f32),
            pltpu.SMEM((1, PEERS), jnp.int32),
            pltpu.SMEM((1, PEERS), jnp.int32),
            dma((7,)),
            dma((2, 2, 7)),
            dma((2, 2, PEERS)),
            dma((head_parts,)),
            dma((head_parts,)),
            dma((PEERS // 2,)),
            dma((PEERS // 2,)),
            dma((PEERS // 2,)),
            dma((PEERS // 2,)),
            dma((7,)),
            dma((PEERS,)),
            dma((7,)),
            dma((PEERS,)),
        ],
        compiler_params=pltpu.CompilerParams(
            collective_id=0, has_side_effects=True, vmem_limit_bytes=40 * 2**20
        ),
        name="fused",
    )(
        *(
            pltpu.with_memory_space_constraint(x, pltpu.HBM)
            for x in (
                queries,
                keys,
                values,
                residual,
                norm_gain.reshape(HEADS, HD),
                block_pos,
                doc_offset,
            )
        )
    )


def solution(mesh):
    peers, head_parts = mesh.shape["seq"], mesh.shape["head"]
    if peers == PEERS and HEADS // head_parts == 2 * PEERS:
        local = functools.partial(local_fused, head_parts)
    else:
        local = local_generic
    return jax.shard_map(
        local,
        mesh=mesh,
        in_specs=(
            P("seq", "head"),
            P("seq", None),
            P("seq", None),
            P("seq", "head"),
            P(),
            P(),
            P(),
        ),
        out_specs=(P("seq", "head"), P("head", None, None), P("seq", "head")),
        check_vma=False,
    )
```

```python
import functools
import math

import jax
import jax.numpy as jnp
from jax import lax
from jax.experimental import pallas as pl
from jax.experimental.pallas import tpu as pltpu
from jax.sharding import PartitionSpec as P

HEADS = 64
KVH = 8
HD = 128
BLOCK = 128
COPIES = 1
WIDTH = 8192


EPSILON = 1e-05


def positions_and_docs(block_pos, doc_offset):
    block_total = block_pos.shape[0]
    doc_flags = (doc_offset < BLOCK).astype(jnp.int32)
    places = jnp.arange(block_total, dtype=jnp.int32)
    earlier = places[:, None] < places[None, :]
    starts_before = jnp.sum(jnp.where(earlier, doc_flags[:, None], 0), axis=0)
    matches = block_pos[:, None] == jnp.arange(block_total, dtype=jnp.int32)[None, :]
    start_count = jnp.sum(jnp.where(matches, starts_before[None, :], 0), axis=1)
    offsets = jnp.sum(jnp.where(matches, doc_offset[None, :], 0), axis=1)
    within = jnp.arange(BLOCK, dtype=jnp.int32)
    seq_pos = (block_pos[:, None] * BLOCK + within[None, :]).reshape(-1)
    doc_id = (
        start_count[:, None] + (within[None, :] >= offsets[:, None]).astype(jnp.int32)
    ).reshape(-1)
    return (seq_pos, doc_id)


HIGHEST = lax.Precision.HIGHEST
MESH = pl.DeviceIdType.MESH
PANEL = 16
LOG2E = 1.4426950408889634


def iota(shape, dimension):
    return lax.broadcasted_iota(jnp.int32, shape, dimension)


def factor(m_ref):
    count = m_ref.shape[0]
    lane = iota((PANEL, HD), 1)
    sub = iota((PANEL, HD), 0)

    def panel(j, carry):
        base = pl.multiple_of(j * PANEL, PANEL)
        rows = pl.ds(base, PANEL)
        left = [m_ref[c, rows, :HD] for c in range(count)]
        right = [m_ref[c, rows, HD:] for c in range(count)]
        columns = [
            [
                jnp.broadcast_to(
                    jnp.sum(jnp.where(lane == base + i, left[c], 0.0), axis=1, keepdims=True),
                    (PANEL, HD),
                )
                for i in range(PANEL)
            ]
            for c in range(count)
        ]
        scale = [jnp.ones((PANEL, HD), jnp.float32) for c in range(count)]
        for i in range(PANEL):
            for c in range(count):
                pivot = columns[c][i][i : i + 1, :]
                scale[c] = jnp.where(sub == i, lax.rsqrt(pivot), scale[c])
                ratio = jnp.where(sub > i, columns[c][i] * (1.0 / pivot), 0.0)
                left[c] = left[c] - ratio * left[c][i : i + 1, :]
                right[c] = right[c] - ratio * right[c][i : i + 1, :]
                for k in range(i + 1, PANEL):
                    columns[c][k] = columns[c][k] - ratio * columns[c][k][i : i + 1, :]
        for c in range(count):
            both = jnp.concatenate([left[c] * scale[c], right[c] * scale[c]], axis=1)
            m_ref[c, rows, :] = both
            later = jnp.where(lane >= base + PANEL, both[:, :HD], 0.0)
            m_ref[c] = m_ref[c] - lax.dot_general(
                later,
                both,
                (((0,), (0,)), ((), ())),
                precision=HIGHEST,
                preferred_element_type=jnp.float32,
            )
        return carry

    lax.fori_loop(0, HD // PANEL, panel, 0, unroll=True)


def split(x):
    high = x.astype(jnp.bfloat16)
    return (high, (x - high.astype(jnp.float32)).astype(jnp.bfloat16))


def product(a, b, dims):
    (a_high, a_low), (b_high, b_low) = split(a), split(b)
    dot = functools.partial(
        lax.dot_general, dimension_numbers=(dims, ((), ())), preferred_element_type=jnp.float32
    )
    return dot(a_high, b_high) + (dot(a_high, b_low) + dot(a_low, b_high))


def pack(m):
    return jnp.where(iota((HD, HD), 1) >= iota((HD, HD), 0), m[:, :HD], m[:, HD:])


def unpack(x):
    row, col = iota((HD, HD), 0), iota((HD, HD), 1)
    upper = jnp.where(col >= row, x, 0.0)
    inverse = jnp.where(col < row, x, jnp.where(col == row, 1.0 / x, 0.0))
    return (upper, inverse)


def identity():
    return jnp.where(iota((HD, HD), 0) == iota((HD, HD), 1), 1.0, 0.0)


def factor_kernel(g_ref, x_ref, m_ref):
    m_ref[0, :, :HD] = g_ref[0]
    m_ref[0, :, HD:] = identity()
    factor(m_ref)
    x_ref[0] = pack(m_ref[0])


def factor_heads(gram):
    spec = pl.BlockSpec((1, HD, HD), lambda h: (h, 0, 0))
    return pl.pallas_call(
        factor_kernel,
        grid=(gram.shape[0],),
        in_specs=[spec],
        out_specs=spec,
        out_shape=jax.ShapeDtypeStruct(gram.shape, jnp.float32),
        scratch_shapes=[pltpu.VMEM((1, HD, 2 * HD), jnp.float32)],
        name="factor_heads",
    )(gram)


def gram_of(matrix):
    return jnp.einsum("hnc,hnd->hcd", matrix, matrix, precision=lax.Precision.HIGHEST)


def local_generic(queries, keys, values, residual, norm_gain, block_pos, doc_offset):
    row_count = queries.shape[0]
    head_count = queries.shape[1] // HD
    group_size = HEADS // KVH
    share_count = max(1, head_count // group_size)
    per_share = head_count // share_count
    total_rows = row_count * lax.axis_size("seq")
    global_first = lax.axis_index("head") * head_count
    copy_index = global_first // HEADS
    first_head = global_first % HEADS
    first_share = first_head // group_size
    key_start = copy_index * (KVH * HD) + first_share * HD
    key_cols = lax.dynamic_slice_in_dim(keys, key_start, share_count * HD, 1)
    value_cols = lax.dynamic_slice_in_dim(values, key_start, share_count * HD, 1)
    own_blocks = lax.dynamic_index_in_dim(block_pos, copy_index, 0, keepdims=False)
    own_offsets = lax.dynamic_index_in_dim(doc_offset, copy_index, 0, keepdims=False)
    gain_cols = lax.dynamic_slice_in_dim(norm_gain, first_head * HD, head_count * HD)
    seq_pos, doc_id = positions_and_docs(own_blocks, own_offsets)
    first_row = lax.axis_index("seq") * row_count
    own_pos = lax.dynamic_slice_in_dim(seq_pos, first_row, row_count)
    own_doc = lax.dynamic_slice_in_dim(doc_id, first_row, row_count)
    query_heads = queries.reshape(row_count, share_count, per_share, HD)
    score_scale = 1.0 / math.sqrt(HD)

    def attend_block(state_now, key_piece, value_piece, first_key):
        length = key_piece.shape[0]
        key_pos = lax.dynamic_slice_in_dim(seq_pos, first_key, length)
        key_doc = lax.dynamic_slice_in_dim(doc_id, first_key, length)
        seen = (key_pos[None, :] <= own_pos[:, None]) & (key_doc[None, :] == own_doc[:, None])

        def accumulate(state_inner):
            run_max, run_total, run_acc = state_inner
            key_heads = key_piece.reshape(length, share_count, HD)
            value_heads = value_piece.reshape(length, share_count, HD)
            scores = (
                jnp.einsum(
                    "rkgd,nkd->kgrn", query_heads, key_heads, preferred_element_type=jnp.float32
                )
                * score_scale
            )
            scores = jnp.where(seen[None, None], scores, -jnp.inf)
            new_max = jnp.maximum(run_max, jnp.max(scores, axis=3))
            factor = jnp.exp(run_max - new_max)
            expo = jnp.exp(scores - new_max[..., None])
            new_total = run_total * factor + jnp.sum(expo, axis=3)
            partial_value = jnp.einsum(
                "kgrn,nkd->kgrd",
                expo.astype(jnp.bfloat16),
                value_heads,
                preferred_element_type=jnp.float32,
            )
            new_acc = run_acc * factor[..., None] + partial_value
            return (new_max, new_total, new_acc)

        def unchanged(state_inner):
            return state_inner

        return lax.cond(jnp.any(seen), accumulate, unchanged, state_now)

    def attend(state_now, pieces, first_key):
        key_piece, value_piece = pieces
        length = key_piece.shape[0]
        step_rows = math.gcd(length, 1024)
        if step_rows == length:
            return attend_block(state_now, key_piece, value_piece, first_key)

        def advance(step_index, state_inner):
            begin_row = step_index * step_rows
            key_part = lax.dynamic_slice_in_dim(key_piece, begin_row, step_rows, 0)
            value_part = lax.dynamic_slice_in_dim(value_piece, begin_row, step_rows, 0)
            return attend_block(state_inner, key_part, value_part, first_key + begin_row)

        return lax.fori_loop(0, length // step_rows, advance, state_now)

    start_state = (
        jnp.full((share_count, per_share, row_count), -1e30, jnp.float32),
        jnp.zeros((share_count, per_share, row_count), jnp.float32),
        jnp.zeros((share_count, per_share, row_count, HD), jnp.float32),
    )
    final_max, final_total, final_acc = attend(
        start_state,
        (
            lax.all_gather(key_cols, "seq", axis=0, tiled=True),
            lax.all_gather(value_cols, "seq", axis=0, tiled=True),
        ),
        jnp.int32(0),
    )
    output = final_acc / final_total[..., None]
    attn_out = (
        jnp.transpose(output, (2, 0, 1, 3)).reshape(row_count, head_count * HD).astype(jnp.bfloat16)
    )
    mixed = attn_out.astype(jnp.float32) + residual.astype(jnp.float32)
    local_squares = jnp.sum(mixed * mixed, axis=1)
    slot_mask = jnp.arange(COPIES, dtype=jnp.int32) == copy_index
    slotted = jnp.where(slot_mask[:, None], local_squares[None, :], 0.0)
    summed = lax.psum(slotted, "head")
    square_sum = lax.dynamic_index_in_dim(summed, copy_index, 0, keepdims=False)
    normed = mixed * lax.rsqrt(square_sum[:, None] / WIDTH + EPSILON) * gain_cols[None, :]
    blocks = normed.reshape(row_count, head_count, HD)
    head_rows = jnp.transpose(blocks, (1, 0, 2))
    gram_sum = lax.psum(gram_of(head_rows), "seq")
    upper, inverse = unpack(factor_heads(gram_sum))
    r_factor = upper / math.sqrt(total_rows)
    whitened = jnp.einsum("rhc,hdc->rhd", blocks, inverse, precision=HIGHEST)
    whitened = whitened.reshape(row_count, head_count * HD) * math.sqrt(total_rows)
    return (attn_out, r_factor, whitened)


PEERS = 8


def fused_kernel(
    heads,
    head_parts,
    q_ref,
    k_ref,
    v_ref,
    res_ref,
    gain_hbm,
    pos_hbm,
    off_hbm,
    attn_buf,
    r_buf,
    white_buf,
    q_buf,
    res_buf,
    k_buf,
    v_buf,
    bias,
    mixed,
    squares,
    g_send,
    g_recv,
    g_half,
    m_ref,
    w_buf,
    u_buf,
    gain_ref,
    pos_ref,
    off_ref,
    local_sem,
    kv_send,
    kv_recv,
    sq_send,
    sq_recv,
    g_send_sem,
    g_recv_sem,
    half_send,
    half_recv,
    w_send,
    w_recv,
    u_send,
    u_recv,
):
    me = lax.axis_index("seq")
    part = lax.axis_index("head")
    group = HEADS // KVH
    shares = heads // group
    width = shares * HD
    core = me % 2
    bit_x = (me // 2) % 2
    bit_y = me // 4
    to_sib = 1 - 2 * core
    to_x = 2 - 4 * bit_x
    to_y = 4 - 8 * bit_y
    sib = me + to_sib
    near = [me + to_x + to_y, me + to_x, me + to_y]

    key_cols = pl.ds(pl.multiple_of(part * width, HD), width)
    own_rows = pl.ds(pl.multiple_of(me * BLOCK, BLOCK), BLOCK)
    loads = [
        pltpu.make_async_copy(k_ref.at[:, key_cols], k_buf.at[own_rows], local_sem.at[0]),
        pltpu.make_async_copy(v_ref.at[:, key_cols], v_buf.at[own_rows], local_sem.at[1]),
        pltpu.make_async_copy(q_ref, q_buf, local_sem.at[2]),
        pltpu.make_async_copy(res_ref, res_buf, local_sem.at[3]),
        pltpu.make_async_copy(pos_hbm, pos_ref, local_sem.at[4]),
        pltpu.make_async_copy(off_hbm, off_ref, local_sem.at[5]),
        pltpu.make_async_copy(gain_hbm, gain_ref, local_sem.at[6]),
    ]
    for copy in loads:
        copy.start()

    barrier = pltpu.get_barrier_semaphore()
    for step in range(1, PEERS):
        pl.semaphore_signal(
            barrier, inc=1, device_id=((me + step) % PEERS, part), device_id_type=MESH
        )
    for step in range(1, head_parts):
        pl.semaphore_signal(
            barrier, inc=1, device_id=(me, (part + step) % head_parts), device_id_type=MESH
        )
    pl.semaphore_wait(barrier, PEERS - 1 + head_parts - 1)

    def remote(src, dst, send, recv, device):
        return pltpu.make_async_remote_copy(
            src_ref=src,
            dst_ref=dst,
            send_sem=send,
            recv_sem=recv,
            device_id=device,
            device_id_type=MESH,
        )

    def spread(slot_of, send, recv):
        copies = []
        for t, peer in enumerate(near + [sib]):
            copy = remote(slot_of(me), slot_of(me), send.at[t], recv.at[me], (peer, part))
            copy.start()
            copies.append(copy)
        return copies

    def arrived(slot_of, send, recv, owner):
        remote(slot_of(owner), slot_of(owner), send.at[0], recv.at[owner], (sib, part)).wait_recv()

    def forward(slot_of, send, recv, t):
        owner = near[t]
        arrived(slot_of, send, recv, owner)
        copy = remote(slot_of(owner), slot_of(owner), send.at[4 + t], recv.at[owner], (sib, part))
        copy.start()
        return copy

    def part_of(buf, share):
        cols = slice(share * HD, (share + 1) * HD)
        return lambda owner: buf.at[pl.ds(pl.multiple_of(owner * BLOCK, BLOCK), BLOCK), cols]

    pending = []
    kv = [
        [
            (part_of(buf, share), kv_send.at[share, i], kv_recv.at[share, i])
            for i, buf in enumerate((k_buf, v_buf))
        ]
        for share in range(shares)
    ]
    loads[0].wait()
    loads[1].wait()
    for ways in kv:
        for way in ways:
            pending += spread(*way)

    def pass_on(share, t):
        for way in kv[share]:
            pending.append(forward(*way, t))

    def complete(share):
        for owner in [sib] + [peer + to_sib for peer in near]:
            for way in kv[share]:
                arrived(*way, owner)

    loads[4].wait()
    loads[5].wait()
    row_pos = pos_ref[0, me]
    lane = iota((BLOCK, BLOCK), 1)
    sub = iota((BLOCK, BLOCK), 0)

    def starts(position):
        total = jnp.int32(0)
        for b in range(PEERS):
            counted = (b < position) & (off_ref[0, b] < BLOCK)
            total = total + jnp.where(counted, 1, 0)
        return total

    own_pos = row_pos * BLOCK + sub
    own_doc = starts(row_pos) + jnp.where(sub >= off_ref[0, row_pos], 1, 0)
    for s in range(PEERS):
        position = pos_ref[0, s]
        key_pos = position * BLOCK + lane
        key_doc = starts(position) + jnp.where(lane >= off_ref[0, position], 1, 0)
        seen = (key_pos <= own_pos) & (key_doc == own_doc)
        bias[:, s * BLOCK : (s + 1) * BLOCK] = jnp.where(seen, 0.0, -jnp.inf)

    for t in (1, 2, 0):
        pass_on(0, t)
    complete(0)
    loads[2].wait()
    loads[3].wait()
    loads[6].wait()

    def attend(h, square):
        cols = pl.ds(pl.multiple_of(h * HD, HD), HD)
        share = pl.ds(pl.multiple_of((h // group) * HD, HD), HD)
        scores = lax.dot_general(
            q_buf[:, cols],
            k_buf[:, share],
            (((1,), (1,)), ((), ())),
            preferred_element_type=jnp.float32,
        )
        scores = scores + bias[...]
        top = jnp.max(scores, axis=1, keepdims=True)
        expo = jnp.exp2((scores - top) * (LOG2E / math.sqrt(HD)))
        total = jnp.sum(expo, axis=1, keepdims=True)
        out = lax.dot_general(
            expo.astype(jnp.bfloat16),
            v_buf[:, share],
            (((1,), (0,)), ((), ())),
            preferred_element_type=jnp.float32,
        )
        out = (out / total).astype(jnp.bfloat16)
        attn_buf[:, cols] = out
        mix = out.astype(jnp.float32) + res_buf[:, cols].astype(jnp.float32)
        mixed[:, cols] = mix
        return square + mix * mix

    square = jnp.zeros((BLOCK, HD), jnp.float32)
    for h in range(group // 2):
        square = attend(h, square)
    pass_on(1, 1)
    pass_on(1, 2)
    for h in range(group // 2, group):
        square = attend(h, square)
    pass_on(1, 0)
    complete(1)
    square = lax.fori_loop(group, heads, attend, square, unroll=4)

    squares[part] = jnp.broadcast_to(jnp.sum(square.T, axis=0, keepdims=True), (8, HD))
    for step in range(1, head_parts):
        copy = remote(
            squares.at[part],
            squares.at[part],
            sq_send.at[step],
            sq_recv.at[part],
            (me, (part + step) % head_parts),
        )
        copy.start()
        pending.append(copy)
    for step in range(1, head_parts):
        other = (part + step) % head_parts
        remote(
            squares.at[other], squares.at[other], sq_send.at[step], sq_recv.at[other], (me, other)
        ).wait_recv()
    total = squares[0]
    for p in range(1, head_parts):
        total = total + squares[p]
    inv_rms = lax.rsqrt(total[0:1, :] / WIDTH + EPSILON)
    inv_rms = jnp.broadcast_to(inv_rms, (BLOCK, HD)).T

    def gram(h):
        cols = pl.ds(pl.multiple_of(h * HD, HD), HD)
        normed = mixed[:, cols] * inv_rms * gain_ref[pl.ds(part * heads + h, 1), :]
        mixed[:, cols] = normed
        return lax.dot_general(
            normed,
            normed,
            (((0,), (0,)), ((), ())),
            precision=HIGHEST,
            preferred_element_type=jnp.float32,
        )

    def make_pair(p, ref):
        first, second = gram(2 * p), gram(2 * p + 1)
        ref[:HD, :] = jnp.where(sub >= lane, first, second)
        diagonal = jnp.sum(jnp.where(sub == lane, second, 0.0), axis=0, keepdims=True)
        ref[HD:, :] = jnp.broadcast_to(diagonal, (8, HD))

    chip = me // 2
    chips = PEERS // 2
    for k in range(1, chips + 1):
        target = (chip + k) % chips
        make_pair(2 * target + 1 - core, g_send.at[target])
        copy = remote(
            g_send.at[target], g_half.at[target], half_send.at[k - 1], half_recv.at[target], (sib, part)
        )
        copy.start()
        pending.append(copy)

    def half(target):
        remote(
            g_half.at[target], g_half.at[target], half_send.at[0], half_recv.at[target], (sib, part)
        ).wait_recv()
        return g_half[target]

    for k in range(1, chips):
        target = (chip + k) % chips
        slot = g_send.at[chips + target]
        make_pair(2 * target + core, slot)
        slot[...] = slot[...] + half(target)
        copy = remote(
            slot, g_recv.at[chip], g_send_sem.at[k], g_recv_sem.at[chip], (2 * target + core, part)
        )
        copy.start()
        pending.append(copy)
    make_pair(me, g_recv.at[chip])
    g_recv[chip] = g_recv[chip] + half(chip)
    for k in range(1, chips):
        source = (chip + k) % chips
        remote(
            g_recv.at[source],
            g_recv.at[source],
            g_send_sem.at[k],
            g_recv_sem.at[source],
            (2 * source + core, part),
        ).wait_recv()
    gram_sum = g_recv[0]
    for c in range(1, chips):
        gram_sum = gram_sum + g_recv[c]
    body = gram_sum[:HD, :]
    turned = body.T
    eye = sub == lane
    m_ref[0, :, :HD] = jnp.where(sub >= lane, body, turned)
    m_ref[1, :, :HD] = jnp.where(
        eye, gram_sum[HD : HD + 1, :], jnp.where(sub < lane, body, turned)
    )
    for c in range(2):
        m_ref[c, :, HD:] = identity()
    factor(m_ref)
    root = math.sqrt(BLOCK * PEERS)

    second = m_ref[1, :, HD:]
    diagonal = jnp.sum(jnp.where(eye, second, 0.0), axis=0, keepdims=True)
    w_buf[me, :HD, :] = jnp.where(sub >= lane, m_ref[0, :, HD:], second.T)
    w_buf[me, HD:, :] = jnp.broadcast_to(diagonal, (8, HD))
    w_way = (lambda owner: w_buf.at[owner], w_send, w_recv)
    pending += spread(*w_way)
    second = m_ref[1, :, :HD]
    diagonal = jnp.sum(jnp.where(eye, second, 0.0), axis=0, keepdims=True)
    pair = jnp.where(sub <= lane, m_ref[0, :, :HD], second.T)
    u_buf[me, :HD, :] = (pair * (1.0 / root)).astype(jnp.bfloat16)
    u_buf[me, HD:, :] = jnp.broadcast_to(diagonal * (1.0 / root), (16, HD)).astype(jnp.bfloat16)
    u_way = (lambda owner: u_buf.at[owner], u_send, u_recv)
    pending += spread(*u_way)

    def whiten(owner):
        body = w_buf[owner, :HD, :]
        diagonal = w_buf[owner, HD : HD + 1, :]
        first = jnp.where(sub >= lane, body, 0.0)
        second = jnp.where(sub < lane, body, jnp.where(eye, diagonal, 0.0))
        for c, (inverse, side) in enumerate(((first, 1), (second, 0))):
            cols = pl.ds(pl.multiple_of((2 * owner + c) * HD, HD), HD)
            white_buf[:, cols] = root * product(mixed[:, cols], inverse, ((1,), (side,)))

    def expand(owner):
        body = u_buf[owner, :HD, :].astype(jnp.float32)
        diagonal = u_buf[owner, HD:, :].astype(jnp.float32)[0:1, :]
        r_buf[2 * owner] = jnp.where(sub <= lane, body, 0.0)
        r_buf[2 * owner + 1] = jnp.where(sub < lane, body.T, jnp.where(eye, diagonal, 0.0))

    whiten(me)
    arrived(*w_way, sib)
    whiten(sib)
    for t in (1, 2, 0):
        pending.append(forward(*w_way, t))
        whiten(near[t])
    expand(me)
    arrived(*u_way, sib)
    expand(sib)
    for t in (1, 2, 0):
        pending.append(forward(*u_way, t))
        arrived(*w_way, near[t] + to_sib)
        whiten(near[t] + to_sib)
        expand(near[t])
    for t in (1, 2, 0):
        arrived(*u_way, near[t] + to_sib)
        expand(near[t] + to_sib)
    for copy in pending:
        copy.wait_send()


def local_fused(head_parts, queries, keys, values, residual, norm_gain, block_pos, doc_offset):
    rows, columns = queries.shape
    heads = columns // HD
    width = heads // (HEADS // KVH) * HD
    f32, bf16 = jnp.float32, jnp.bfloat16
    outside = pl.BlockSpec(memory_space=pltpu.HBM)
    inside = pl.BlockSpec(memory_space=pltpu.VMEM)
    dma = pltpu.SemaphoreType.DMA
    return pl.pallas_call(
        functools.partial(fused_kernel, heads, head_parts),
        in_specs=[outside] * 7,
        out_specs=(inside,) * 3,
        out_shape=(
            jax.ShapeDtypeStruct((rows, columns), bf16),
            jax.ShapeDtypeStruct((heads, HD, HD), f32),
            jax.ShapeDtypeStruct((rows, columns), f32),
        ),
        scratch_shapes=[
            pltpu.VMEM((rows, columns), bf16),
            pltpu.VMEM((rows, columns), bf16),
            pltpu.VMEM((PEERS * BLOCK, width), bf16),
            pltpu.VMEM((PEERS * BLOCK, width), bf16),
            pltpu.VMEM((BLOCK, PEERS * BLOCK), f32),
            pltpu.VMEM((rows, columns), f32),
            pltpu.VMEM((head_parts, 8, HD), f32),
            pltpu.VMEM((PEERS, HD + 8, HD), f32),
            pltpu.VMEM((PEERS // 2, HD + 8, HD), f32),
            pltpu.VMEM((PEERS // 2, HD + 8, HD), f32),
            pltpu.VMEM((2, HD, 2 * HD), f32),
            pltpu.VMEM((PEERS, HD + 8, HD), f32),
            pltpu.VMEM((PEERS, HD + 16, HD), bf16),
            pltpu.VMEM((HEADS, HD), f32),
            pltpu.SMEM((1, PEERS), jnp.int32),
            pltpu.SMEM((1, PEERS), jnp.int32),
            dma((7,)),
            dma((2, 2, 7)),
            dma((2, 2, PEERS)),
            dma((head_parts,)),
            dma((head_parts,)),
            dma((PEERS // 2,)),
            dma((PEERS // 2,)),
            dma((PEERS // 2,)),
            dma((PEERS // 2,)),
            dma((7,)),
            dma((PEERS,)),
            dma((7,)),
            dma((PEERS,)),
        ],
        compiler_params=pltpu.CompilerParams(
            collective_id=0, has_side_effects=True, vmem_limit_bytes=40 * 2**20
        ),
        name="fused",
    )(
        *(
            pltpu.with_memory_space_constraint(x, pltpu.HBM)
            for x in (
                queries,
                keys,
                values,
                residual,
                norm_gain.reshape(HEADS, HD),
                block_pos,
                doc_offset,
            )
        )
    )


def solution(mesh):
    peers, head_parts = mesh.shape["seq"], mesh.shape["head"]
    if peers == PEERS and HEADS // head_parts == 2 * PEERS:
        local = functools.partial(local_fused, head_parts)
    else:
        local = local_generic
    return jax.shard_map(
        local,
        mesh=mesh,
        in_specs=(
            P("seq", "head"),
            P("seq", None),
            P("seq", None),
            P("seq", "head"),
            P(),
            P(),
            P(),
        ),
        out_specs=(P("seq", "head"), P("head", None, None), P("seq", "head")),
        check_vma=False,
    )
```
